1024 devices in a mesh: seq: 64 (over z, core), head: 16 (over x, y).
Axes of the slice: x: 4, y: 4, z: 32, core: 2. Of those that a mesh axis runs over, the one named last changes fastest.
Arguments:
- queries_first: bfloat16 [8192, 8192], P('seq', 'head'), may hold values from -6 to 6
- keys_first: bfloat16 [8192, 8192], P('seq', 'head'), may hold values from -6 to 6
- values_first: bfloat16 [8192, 8192], P('seq', 'head'), may hold values from -6 to 6
- queries_second: bfloat16 [8192, 8192], P('seq', 'head'), may hold values from -6 to 6
- rates: float32 [16, 8192], P('head', 'seq'), may hold values from 0.05 to 1
- gate_memory: bfloat16 [16, 512, 512], P('head'), may hold values from -0.25 to 0.25
- up_memory: bfloat16 [16, 512, 512], P('head'), may hold values from -0.25 to 0.25
- down_memory: bfloat16 [16, 512, 512], P('head'), may hold values from -0.25 to 0.25
- out_proj: bfloat16 [8192, 512], P('head'), may hold values from -0.0625 to 0.0625
Outputs:
- projected: bfloat16 [8192, 1024], P(('seq', 'head'))
The draws below stay inside these ranges and needn't reach their ends.
All inputs are finite; a program needn't handle non-finite values.
Results may differ from the reference program's by a relative error of at most 0.018.
Values may be sent and summed in bfloat16 or wider, within the bound.
No kernel may reach another device: no remote copies, remote signals or barrier semaphores. Data moves between devices by JAX's collectives and lax.ppermute only.
A program may use at most 32 MiB of HBM per device.

```python
import math
import jax
import jax.numpy as jnp
from jax import lax

DH = 512
HF = 512
DS = 512
NS_ITERS = 2
HEADS = 16
TOKENS = 8192


def block_scale(key, extent, shards, low, high):
    def one(axis_at, parts):
        draws = jax.random.uniform(jax.random.fold_in(jax.random.fold_in(key, 6), axis_at), (parts,), jnp.float32, low / len(shards), high / len(shards))
        return jnp.repeat(jnp.exp(draws), extent[axis_at] // parts).reshape((-1,) + (1,) * (len(extent) - axis_at - 1))

    loudness = one(*shards[0])
    for cut in shards[1:]:
        loudness = loudness * one(*cut)
    return loudness


def noise(rng, shape, deviation, reach, cuts=(), kind=jnp.bfloat16):
    loudness = block_scale(rng, shape, cuts, -0.22, 0.18) if cuts else 1.0
    result = jax.random.normal(rng, shape, jnp.float32) * deviation * loudness
    return jnp.minimum(jnp.maximum(result, -reach), reach).astype(kind)


def setup_inputs(seed: int = 0) -> dict:
    key_of = jax.random.split(jax.random.key(seed), 10)
    return {
        "queries_first": noise(key_of[0], (TOKENS, HEADS * DH), 1.0, 6.0, ((0, 64), (1, 16))),
        "keys_first": noise(key_of[1], (TOKENS, HEADS * DH), 1.0, 6.0, ((0, 64), (1, 16))),
        "values_first": noise(key_of[2], (TOKENS, HEADS * DH), 1.0, 6.0, ((0, 64), (1, 16))),
        "queries_second": noise(key_of[3], (TOKENS, HEADS * DH), 1.0, 6.0, ((0, 64), (1, 16))),
        "rates": jnp.clip(jnp.exp(math.log(1.0) - 2.9957323 * jax.random.uniform(key_of[4], (HEADS, TOKENS), jnp.float32) ** block_scale(key_of[4], (HEADS, TOKENS), ((0, 16), (1, 64)), -0.2, 0.2)), 0.05, 1.0),
        "gate_memory": noise(key_of[5], (HEADS, DH, HF), DH ** -0.5, 0.25, ((0, 16),)),
        "up_memory": noise(key_of[6], (HEADS, DH, HF), DH ** -0.5, 0.25, ((0, 16),)),
        "down_memory": noise(key_of[7], (HEADS, HF, DH), HF ** -0.5, 0.25, ((0, 16),)),
        "out_proj": noise(key_of[8], (HEADS * DH, DS), (HEADS * DH) ** -0.5, 0.0625, ((0, 16),)),
    }


first_coeff = 3.4445
second_coeff = -4.775
third_coeff = 2.0315
step_scale = 0.5

def apply_memory(inputs, w_gate, w_up, w_down):
    gating = jnp.dot(inputs, w_gate, preferred_element_type=jnp.float32)
    lifted = jnp.dot(inputs, w_up, preferred_element_type=jnp.float32)
    hidden = (jax.nn.silu(gating) * lifted).astype(jnp.bfloat16)
    return jnp.dot(hidden, w_down, preferred_element_type=jnp.float32).astype(jnp.bfloat16)

def descents(key_rows, value_rows, rate_row, w_gate, w_up, w_down):
    gating = jnp.dot(key_rows, w_gate, preferred_element_type=jnp.float32)
    lifted = jnp.dot(key_rows, w_up, preferred_element_type=jnp.float32)
    sigmoid_gate = jax.nn.sigmoid(gating)
    activated = gating * sigmoid_gate
    hidden = (activated * lifted).astype(jnp.bfloat16)
    scaled = (rate_row[:, None] * value_rows.astype(jnp.float32)).astype(jnp.bfloat16)
    backward = jnp.dot(scaled, w_down.T, preferred_element_type=jnp.float32)
    gate_back = (backward * lifted * sigmoid_gate * (1.0 + gating * (1.0 - sigmoid_gate))).astype(jnp.bfloat16)
    up_back = (backward * activated).astype(jnp.bfloat16)
    return (jnp.dot(key_rows.T, gate_back, preferred_element_type=jnp.float32), jnp.dot(key_rows.T, up_back, preferred_element_type=jnp.float32), jnp.dot(scaled.T, hidden, preferred_element_type=jnp.float32))

def orthogonalize(matrix):
    widened = matrix.astype(jnp.float32)
    magnitude = jnp.sqrt(jnp.sum(widened * widened)) + 1e-07
    current = (widened / magnitude).astype(jnp.bfloat16)
    for step in range(NS_ITERS):
        gram_matrix = lax.optimization_barrier(jnp.dot(current, current.T, preferred_element_type=jnp.float32).astype(jnp.bfloat16))
        square = jnp.dot(gram_matrix, gram_matrix, preferred_element_type=jnp.float32)
        polynomial = (second_coeff * gram_matrix.astype(jnp.float32) + third_coeff * square).astype(jnp.bfloat16)
        mixed = jnp.dot(polynomial, current, preferred_element_type=jnp.float32)
        current = (first_coeff * current.astype(jnp.float32) + mixed).astype(jnp.bfloat16)
    return current

def updated(memory, direction):
    return (memory.astype(jnp.float32) + step_scale * direction.astype(jnp.float32)).astype(jnp.bfloat16)

def reference(queries_first, keys_first, values_first, queries_second, rates, gate_memory, up_memory, down_memory, out_proj):

    def one_head(head_index):
        offset = (head_index * DH).astype(jnp.int32)
        query_one = lax.dynamic_slice_in_dim(queries_first, offset, DH, 1)
        key_rows = lax.dynamic_slice_in_dim(keys_first, offset, DH, 1)
        value_rows = lax.dynamic_slice_in_dim(values_first, offset, DH, 1)
        query_two = lax.dynamic_slice_in_dim(queries_second, offset, DH, 1)
        rate_row = lax.dynamic_index_in_dim(rates, head_index, 0, keepdims=False)
        w_gate = lax.dynamic_index_in_dim(gate_memory, head_index, 0, keepdims=False)
        w_up = lax.dynamic_index_in_dim(up_memory, head_index, 0, keepdims=False)
        w_down = lax.dynamic_index_in_dim(down_memory, head_index, 0, keepdims=False)
        first_out = apply_memory(query_one, w_gate, w_up, w_down)
        gate_sum, up_sum, down_sum = descents(key_rows, value_rows, rate_row, w_gate, w_up, w_down)
        new_gate = updated(w_gate, orthogonalize(gate_sum.astype(jnp.bfloat16)))
        new_up = updated(w_up, orthogonalize(up_sum.astype(jnp.bfloat16)))
        new_down = updated(w_down, orthogonalize(down_sum.astype(jnp.bfloat16)).T)
        second_out = apply_memory(query_two, new_gate, new_up, new_down)
        return (first_out, second_out)
    first_all, second_all = lax.map(one_head, jnp.arange(HEADS, dtype=jnp.int32))
    first_flat = jnp.transpose(first_all, (1, 0, 2)).reshape(TOKENS, HEADS * DH)
    second_flat = jnp.transpose(second_all, (1, 0, 2)).reshape(TOKENS, HEADS * DH)
    first_proj = jnp.dot(first_flat, out_proj, preferred_element_type=jnp.float32)
    second_proj = jnp.dot(second_flat, out_proj, preferred_element_type=jnp.float32)
    return jnp.concatenate([first_proj, second_proj], axis=1).astype(jnp.bfloat16)
```

```python
import jax
import jax.numpy as jnp
from jax import lax
from jax.sharding import Mesh
from jax.sharding import PartitionSpec as P

NS_ITERS = 2
FAR, NEAR, CORES, SIDE = 8, 4, 2, 4
ROWS = 8

first_coeff = 3.4445
second_coeff = -4.775
third_coeff = 2.0315
step_scale = 0.5

f32 = jnp.float32
bf16 = jnp.bfloat16
SWAP = [(0, 1), (1, 0)]


def dot(a, b, contract):
    return lax.dot_general(a, b, ((contract[:1], contract[1:]), ((), ())), preferred_element_type=f32)


def apply_memory(inputs, w_gate, w_up, w_down, side):
    gating = dot(inputs, w_gate, (1, side))
    lifted = dot(inputs, w_up, (1, side))
    hidden = (jax.nn.silu(gating) * lifted).astype(bf16)
    return dot(hidden, w_down, (1, 0)).astype(bf16)


def orthogonalize_transposed(matrix):
    widened = matrix.astype(f32)
    magnitude = jnp.sqrt(jnp.sum(widened * widened)) + 1e-07
    current = (widened / magnitude).astype(bf16)
    for step in range(NS_ITERS):
        gram = dot(current, current, (0, 0)).astype(bf16)
        square = dot(gram, gram, (1, 0))
        polynomial = (second_coeff * gram.astype(f32) + third_coeff * square).astype(bf16)
        mixed = dot(current, polynomial, (1, 0))
        current = (first_coeff * current.astype(f32) + mixed).astype(bf16)
    return current


def updated(memory, direction):
    return (memory.astype(f32) + step_scale * direction.astype(f32)).astype(bf16)


def head_sum(share):
    pieces = lax.all_to_all(share, ("x", "y"), 0, 0, tiled=True)
    pieces = pieces.reshape(SIDE * SIDE, -1, share.shape[1])
    return jnp.sum(pieces.astype(f32), axis=0)


def on_device(q_first, keys, values, q_second, rates, gate_memory, up_memory, down_memory, out_proj):
    core = lax.axis_index("core")
    near = lax.axis_index("near")
    w_gate, w_up, w_down = gate_memory[0], up_memory[0], down_memory[0]
    tokens, width = keys.shape
    gate_t, up_t = w_gate.T, w_up.T

    scaled = (rates[0][:, None] * values.astype(f32)).astype(bf16)
    all_keys = lax.all_gather(keys, "near", axis=0, tiled=True)
    all_scaled = lax.all_gather(scaled, "near", axis=0, tiled=True)

    def share(w):
        rows = w.reshape(CORES, NEAR, FAR * ROWS, width)
        return lax.dynamic_index_in_dim(rows, near, 1, keepdims=False).reshape(-1, width)

    gating = dot(share(gate_t), all_keys, (1, 1))
    lifted = dot(share(up_t), all_keys, (1, 1))
    s = jax.nn.sigmoid(gating)
    activated = gating * s
    hidden = (activated * lifted).astype(bf16)
    backward = dot(share(w_down), all_scaled, (1, 1))
    gate_back = (backward * lifted * s * (1.0 + gating * (1.0 - s))).astype(bf16)
    up_back = (backward * activated).astype(bf16)
    partial = jnp.stack(
        [
            dot(gate_back, all_keys, (1, 0)),
            dot(up_back, all_keys, (1, 0)),
            dot(hidden, all_scaled, (1, 0)),
        ]
    ).reshape(3, CORES, FAR, ROWS, width)
    kept = jnp.where(core == 0, partial[:, 0], partial[:, 1])
    given = jnp.where(core == 0, partial[:, 1], partial[:, 0]).astype(bf16)
    taken = lax.ppermute(given, "core", SWAP)
    pieces = (kept + taken.astype(f32)).astype(bf16).transpose(1, 0, 2, 3)
    pieces = lax.all_to_all(pieces, "far", 0, 0, tiled=True)
    summed = jnp.sum(pieces.astype(f32), axis=0).astype(bf16)
    own = lax.all_gather(summed, "far", axis=0, tiled=False)
    own = lax.all_gather(own, "near", axis=0, tiled=False)
    other = lax.ppermute(own, "core", SWAP)
    halves = jnp.stack([jnp.where(core == 0, own, other), jnp.where(core == 0, other, own)])
    matrices = halves.transpose(3, 0, 1, 2, 4, 5).reshape(3, -1, width)

    results = [orthogonalize_transposed(matrices[m]) for m in range(3)]
    new_gate = updated(gate_t, results[0])
    new_up = updated(up_t, results[1])
    new_down = updated(w_down, results[2])
    first_out = apply_memory(q_first, w_gate, w_up, w_down, 0)
    second_out = apply_memory(q_second, new_gate, new_up, new_down, 1)
    both = jnp.concatenate(
        [dot(first_out, out_proj, (1, 0)), dot(second_out, out_proj, (1, 0))], axis=1
    ).astype(bf16)
    return head_sum(both).astype(bf16)


def solution(mesh):
    fine = Mesh(
        mesh.devices.reshape(FAR, NEAR, CORES, SIDE, SIDE), ("far", "near", "core", "x", "y")
    )
    seq, head = ("far", "near", "core"), ("x", "y")
    in_specs = (
        P(seq, head),
        P(seq, head),
        P(seq, head),
        P(seq, head),
        P(head, seq),
        P(head, None, None),
        P(head, None, None),
        P(head, None, None),
        P(head, None),
    )
    out_specs = P(seq + head, None)
    return jax.shard_map(
        on_device, mesh=fine, in_specs=in_specs, out_specs=out_specs, check_vma=False
    )
```

```python
import jax
import jax.numpy as jnp
from jax import lax
from jax.experimental import pallas as pl
from jax.experimental.pallas import tpu as pltpu
from jax.sharding import Mesh
from jax.sharding import PartitionSpec as P

NS_ITERS = 2
FAR, NEAR, CORES, SIDE = 8, 4, 2, 4
VMEM_BYTES = 48 * 1024 * 1024

first_coeff = 3.4445
second_coeff = -4.775
third_coeff = 2.0315
step_scale = 0.5

f32 = jnp.float32
bf16 = jnp.bfloat16
SWAP = [(0, 1), (1, 0)]


def dot(a, b, contract=(1, 0)):
    return lax.dot_general(a, b, ((contract[:1], contract[1:]), ((), ())), preferred_element_type=f32)


def swiglu(gating, lifted):
    return (gating * jax.nn.sigmoid(gating) * lifted).astype(bf16)


def first_kernel(q_ref, gate_ref, up_ref, down_ref, proj_ref, share_ref, gate_t_ref, up_t_ref):
    hidden = swiglu(dot(q_ref[...], gate_ref[0]), dot(q_ref[...], up_ref[0]))
    out = dot(hidden, down_ref[0]).astype(bf16)
    share_ref[...] = dot(out, proj_ref[...]).astype(bf16)
    gate_t_ref[...] = gate_ref[0].T
    up_t_ref[...] = up_ref[0].T


def descent_kernel(place_ref, tokens_ref, gate_ref, up_ref, down_ref, kept_ref, given_ref, sums):
    core, near = place_ref[0], place_ref[1]
    rows = tokens_ref.shape[1] // 2
    part = gate_ref.shape[2] // NEAR
    half = part // CORES
    columns = pl.ds(pl.multiple_of(near * part, part), part)
    keys = jnp.concatenate([tokens_ref[i, :rows] for i in range(NEAR)], axis=0)
    scaled = jnp.concatenate([tokens_ref[i, rows:] for i in range(NEAR)], axis=0)
    gating = dot(gate_ref[0, :, columns].T, keys, (1, 1))
    lifted = dot(up_ref[0, :, columns].T, keys, (1, 1))
    backward = dot(down_ref[0, columns, :], scaled, (1, 1))
    s = jax.nn.sigmoid(gating)
    activated = gating * s
    hidden = (activated * lifted).astype(bf16)
    gate_back = (backward * lifted * s * (1.0 + gating * (1.0 - s))).astype(bf16)
    up_back = (backward * activated).astype(bf16)
    sums[0] = dot(gate_back, keys)
    sums[1] = dot(up_back, keys)
    sums[2] = dot(hidden, scaled)
    mine = pl.ds(pl.multiple_of(core * half, half), half)
    others = pl.ds(pl.multiple_of((1 - core) * half, half), half)
    for m in range(3):
        kept_ref[m * half : (m + 1) * half] = sums[m, mine, :]
        given_ref[m * half : (m + 1) * half] = sums[m, others, :].astype(bf16)


def second_kernel(
    place_ref, own_ref, other_ref, q_ref, gate_t_ref, up_t_ref, down_ref, proj_ref, first_ref, share_ref, work
):
    core = place_ref[0]
    width = q_ref.shape[1]
    part = width // NEAR
    half = part // CORES
    for m in range(3):
        for i in range(NEAR):
            mine = pl.ds(pl.multiple_of(i * part + core * half, half), half)
            others = pl.ds(pl.multiple_of(i * part + (1 - core) * half, half), half)
            work[m, mine, :] = own_ref[i, m * half : (m + 1) * half]
            work[m, others, :] = other_ref[i, m * half : (m + 1) * half]
    for m in range(3):
        widened = work[m].astype(f32)
        magnitude = jnp.sqrt(jnp.sum(widened * widened, keepdims=True)) + 1e-07
        work[m] = (widened / magnitude).astype(bf16)
    for step in range(NS_ITERS):
        for m in range(3):
            current = work[m]
            gram = dot(current, current, (1, 1)).astype(bf16)
            square = dot(gram, gram)
            polynomial = (second_coeff * gram.astype(f32) + third_coeff * square).astype(bf16)
            mixed = dot(polynomial, current)
            work[m] = (first_coeff * current.astype(f32) + mixed).astype(bf16)

    def updated(memory, m):
        return (memory.astype(f32) + step_scale * work[m].astype(f32)).astype(bf16)

    q = q_ref[...]
    gating = dot(q, updated(gate_t_ref[...], 0), (1, 1))
    lifted = dot(q, updated(up_t_ref[...], 1), (1, 1))
    out = dot(swiglu(gating, lifted), updated(down_ref[0], 2)).astype(bf16)
    share_ref[:, :width] = first_ref[...]
    share_ref[:, width:] = dot(out, proj_ref[...]).astype(bf16)


def local(kernel, outs, n_in, scalars, scratch, flops):
    whole = pl.BlockSpec(memory_space=pltpu.VMEM)
    smem = pl.BlockSpec(memory_space=pltpu.SMEM)
    return pl.pallas_call(
        kernel,
        out_shape=[jax.ShapeDtypeStruct(shape, kind) for shape, kind in outs],
        in_specs=[smem] * scalars + [whole] * n_in,
        out_specs=[whole] * len(outs),
        scratch_shapes=scratch,
        compiler_params=pltpu.CompilerParams(vmem_limit_bytes=VMEM_BYTES),
        cost_estimate=pl.CostEstimate(flops=flops, bytes_accessed=3 << 20, transcendentals=0),
    )


def on_device(q_first, keys, values, q_second, rates, gate_memory, up_memory, down_memory, out_proj):
    core = lax.axis_index("core")
    near = lax.axis_index("near")
    place = jnp.stack([core, near]).astype(jnp.int32)
    tokens, width = keys.shape
    unit = width * width

    scaled = (rates[0][:, None] * values.astype(f32)).astype(bf16)
    mine = jnp.concatenate([keys, scaled], axis=0)
    tiles = lax.all_to_all(
        jnp.broadcast_to(mine[None], (NEAR,) + mine.shape), "near", 0, 0, tiled=True
    )
    rows = 3 * width // NEAR // CORES
    kept, given = local(
        descent_kernel,
        [((rows, width), f32), ((rows, width), bf16)],
        4,
        1,
        [pltpu.VMEM((3, width // NEAR, width), f32)],
        12 * tokens * unit,
    )(place, tiles, gate_memory, up_memory, down_memory)
    taken = lax.ppermute(given, "core", SWAP)
    pieces = (kept + taken.astype(f32)).astype(bf16)
    pieces = lax.all_to_all(pieces, "far", 0, 0, tiled=True)
    summed = jnp.sum(pieces.reshape(FAR, -1, width).astype(f32), axis=0).astype(bf16)
    own = lax.all_gather(summed, "far", axis=0, tiled=True)
    own = lax.all_gather(own, "near", axis=0, tiled=False)
    other = lax.ppermute(own, "core", SWAP)
    first_share, gate_t, up_t = local(
        first_kernel,
        [((tokens, width), bf16), ((width, width), bf16), ((width, width), bf16)],
        5,
        0,
        [],
        8 * tokens * unit,
    )(q_first, gate_memory, up_memory, down_memory, out_proj)
    (share,) = local(
        second_kernel,
        [((tokens, 2 * width), bf16)],
        8,
        1,
        [pltpu.VMEM((3, width, width), bf16)],
        36 * width * unit,
    )(place, own, other, q_second, gate_t, up_t, down_memory, out_proj, first_share)
    shares = lax.all_to_all(share, ("x", "y"), 0, 0, tiled=True)
    shares = shares.reshape(SIDE * SIDE, -1, 2 * width)
    return jnp.sum(shares.astype(f32), axis=0).astype(bf16)


def solution(mesh):
    fine = Mesh(
        mesh.devices.reshape(FAR, NEAR, CORES, SIDE, SIDE), ("far", "near", "core", "x", "y")
    )
    seq, head = ("far", "near", "core"), ("x", "y")
    in_specs = (
        P(seq, head),
        P(seq, head),
        P(seq, head),
        P(seq, head),
        P(head, seq),
        P(head, None, None),
        P(head, None, None),
        P(head, None, None),
        P(head, None),
    )
    out_specs = P(seq + head, None)
    return jax.shard_map(
        on_device, mesh=fine, in_specs=in_specs, out_specs=out_specs, check_vma=False
    )
```

```python
import jax
import jax.numpy as jnp
from jax import lax
from jax.experimental import pallas as pl
from jax.experimental.pallas import tpu as pltpu
from jax.sharding import Mesh
from jax.sharding import PartitionSpec as P

NS_ITERS = 2
FAR, MID, PAIR, CORES, SIDE = 4, 4, 2, 2, 4
VMEM_BYTES = 48 * 1024 * 1024

first_coeff = 3.4445
second_coeff = -4.775
third_coeff = 2.0315
step_scale = 0.5

f32 = jnp.float32
bf16 = jnp.bfloat16
SWAP = [(0, 1), (1, 0)]


def dot(a, b, contract=(1, 0)):
    return lax.dot_general(a, b, ((contract[:1], contract[1:]), ((), ())), preferred_element_type=f32)


def swiglu(gating, lifted):
    return (gating * jax.nn.sigmoid(gating) * lifted).astype(bf16)


def first_kernel(q_ref, gate_ref, up_ref, down_ref, proj_ref, share_ref, gate_t_ref, up_t_ref):
    hidden = swiglu(dot(q_ref[...], gate_ref[0]), dot(q_ref[...], up_ref[0]))
    out = dot(hidden, down_ref[0]).astype(bf16)
    share_ref[...] = dot(out, proj_ref[...]).astype(bf16)
    gate_t_ref[...] = gate_ref[0].T
    up_t_ref[...] = up_ref[0].T


def descent_kernel(
    place_ref, keys_a, keys_b, scaled_a, scaled_b, gate_t_ref, up_t_ref, down_ref, kept_ref, given_ref, sums
):
    core, pair = place_ref[0], place_ref[1]
    part = down_ref.shape[1] // PAIR
    half = part // CORES
    units = pl.ds(pl.multiple_of(pair * part, part), part)
    keys = jnp.concatenate([keys_a[...], keys_b[...]], axis=0)
    scaled = jnp.concatenate([scaled_a[...], scaled_b[...]], axis=0)
    gating = dot(gate_t_ref[units, :], keys, (1, 1))
    lifted = dot(up_t_ref[units, :], keys, (1, 1))
    backward = dot(down_ref[0, units, :], scaled, (1, 1))
    s = jax.nn.sigmoid(gating)
    activated = gating * s
    hidden = (activated * lifted).astype(bf16)
    gate_back = (backward * lifted * s * (1.0 + gating * (1.0 - s))).astype(bf16)
    up_back = (backward * activated).astype(bf16)
    sums[0] = dot(gate_back, keys)
    sums[1] = dot(up_back, keys)
    sums[2] = dot(hidden, scaled)
    mine = pl.ds(pl.multiple_of(core * half, half), half)
    others = pl.ds(pl.multiple_of((1 - core) * half, half), half)
    for m in range(3):
        kept_ref[m * half : (m + 1) * half] = sums[m, mine, :]
        given_ref[m * half : (m + 1) * half] = sums[m, others, :].astype(bf16)


def second_kernel(
    place_ref, a_ref, b_ref, c_ref, d_ref, q_ref, gate_t_ref, up_t_ref, down_ref, proj_ref, first_ref, share_ref, work
):
    core, pair = place_ref[0], place_ref[1]
    width = q_ref.shape[1]
    part = width // PAIR
    half = part // CORES
    for ref, other_pair, other_core in ((a_ref, 0, 0), (b_ref, 1, 0), (c_ref, 0, 1), (d_ref, 1, 1)):
        at_pair = 1 - pair if other_pair else pair
        at_core = 1 - core if other_core else core
        at = pl.ds(pl.multiple_of(at_pair * part + at_core * half, half), half)
        for m in range(3):
            work[m, at, :] = ref[m * half : (m + 1) * half]
    for m in range(3):
        widened = work[m].astype(f32)
        magnitude = jnp.sqrt(jnp.sum(widened * widened, keepdims=True)) + 1e-07
        work[m] = (widened / magnitude).astype(bf16)
    for step in range(NS_ITERS):
        for m in range(3):
            current = work[m]
            gram = dot(current, current, (1, 1)).astype(bf16)
            square = dot(gram, gram)
            polynomial = (second_coeff * gram.astype(f32) + third_coeff * square).astype(bf16)
            mixed = dot(polynomial, current)
            work[m] = (first_coeff * current.astype(f32) + mixed).astype(bf16)

    def updated(memory, m):
        return (memory.astype(f32) + step_scale * work[m].astype(f32)).astype(bf16)

    q = q_ref[...]
    gating = dot(q, updated(gate_t_ref[...], 0), (1, 1))
    lifted = dot(q, updated(up_t_ref[...], 1), (1, 1))
    out = dot(swiglu(gating, lifted), updated(down_ref[0], 2)).astype(bf16)
    share_ref[:, :width] = first_ref[...]
    share_ref[:, width:] = dot(out, proj_ref[...]).astype(bf16)


def local(kernel, outs, n_in, scalars, scratch, flops):
    whole = pl.BlockSpec(memory_space=pltpu.VMEM)
    smem = pl.BlockSpec(memory_space=pltpu.SMEM)
    return pl.pallas_call(
        kernel,
        out_shape=[jax.ShapeDtypeStruct(shape, kind) for shape, kind in outs],
        in_specs=[smem] * scalars + [whole] * n_in,
        out_specs=[whole] * len(outs),
        scratch_shapes=scratch,
        compiler_params=pltpu.CompilerParams(vmem_limit_bytes=VMEM_BYTES),
        cost_estimate=pl.CostEstimate(flops=flops, bytes_accessed=3 << 20, transcendentals=0),
    )


def on_device(q_first, keys, values, q_second, rates, gate_memory, up_memory, down_memory, out_proj):
    core = lax.axis_index("core")
    pair = lax.axis_index("pair")
    place = jnp.stack([core, pair]).astype(jnp.int32)
    tokens, width = keys.shape
    unit = width * width

    keys_next = lax.ppermute(keys, "pair", SWAP)
    scaled = (rates[0][:, None] * values.astype(f32)).astype(bf16)
    scaled_next = lax.ppermute(scaled, "pair", SWAP)
    first_share, gate_t, up_t = local(
        first_kernel,
        [((tokens, width), bf16), ((width, width), bf16), ((width, width), bf16)],
        5,
        0,
        [],
        8 * tokens * unit,
    )(q_first, gate_memory, up_memory, down_memory, out_proj)
    rows = 3 * width // PAIR // CORES
    kept, given = local(
        descent_kernel,
        [((rows, width), f32), ((rows, width), bf16)],
        7,
        1,
        [pltpu.VMEM((3, width // PAIR, width), f32)],
        12 * tokens * unit,
    )(place, keys, keys_next, scaled, scaled_next, gate_t, up_t, down_memory)
    taken = lax.ppermute(given, "core", SWAP)
    pieces = (kept + taken.astype(f32)).astype(bf16)
    pieces = lax.all_to_all(pieces, "mid", 0, 0, tiled=True).reshape(MID, -1, width)
    summed = jnp.sum(pieces.astype(f32), axis=0).astype(bf16)
    groups = lax.all_gather(summed, "far", axis=0, tiled=False)
    summed = jnp.sum(groups.astype(f32), axis=0).astype(bf16)
    part_a = lax.all_to_all(
        jnp.broadcast_to(summed[None], (MID,) + summed.shape), "mid", 0, 0, tiled=True
    ).reshape(rows, width)
    part_b = lax.ppermute(part_a, "pair", SWAP)
    part_c = lax.ppermute(part_a, "core", SWAP)
    part_d = lax.ppermute(part_b, "core", SWAP)
    (share,) = local(
        second_kernel,
        [((tokens, 2 * width), bf16)],
        10,
        1,
        [pltpu.VMEM((3, width, width), bf16)],
        36 * width * unit,
    )(place, part_a, part_b, part_c, part_d, q_second, gate_t, up_t, down_memory, out_proj, first_share)
    shares = lax.all_to_all(share, ("x", "y"), 0, 0, tiled=True)
    shares = shares.reshape(SIDE * SIDE, -1, 2 * width)
    return jnp.sum(shares.astype(f32), axis=0).astype(bf16)


def solution(mesh):
    fine = Mesh(
        mesh.devices.reshape(FAR, MID, PAIR, CORES, SIDE, SIDE),
        ("far", "mid", "pair", "core", "x", "y"),
    )
    seq, head = ("far", "mid", "pair", "core"), ("x", "y")
    in_specs = (
        P(seq, head),
        P(seq, head),
        P(seq, head),
        P(seq, head),
        P(head, seq),
        P(head, None, None),
        P(head, None, None),
        P(head, None, None),
        P(head, None),
    )
    out_specs = P(seq + head, None)
    return jax.shard_map(
        on_device, mesh=fine, in_specs=in_specs, out_specs=out_specs, check_vma=False
    )
```

```python
import math

import jax
import jax.numpy as jnp
from jax import lax
from jax.experimental import pallas as pl
from jax.experimental.pallas import tpu as pltpu
from jax.sharding import Mesh
from jax.sharding import PartitionSpec as P

NS_ITERS = 2
FAR, HIGH, LOW, PAIR, CORES, SIDE = 4, 2, 2, 2, 2, 4
VMEM_BYTES = 48 * 1024 * 1024

first_coeff = 3.4445
second_coeff = -4.775
third_coeff = 2.0315
step_scale = 0.5

f32 = jnp.float32
bf16 = jnp.bfloat16
SWAP = [(0, 1), (1, 0)]


def dot(a, b, contract=(1, 0)):
    return lax.dot_general(a, b, ((contract[:1], contract[1:]), ((), ())), preferred_element_type=f32)


def swiglu(gating, lifted):
    return (gating * jax.nn.sigmoid(gating) * lifted).astype(bf16)


def first_kernel(q_ref, gate_ref, up_ref, down_ref, proj_ref, share_ref, gate_t_ref, up_t_ref):
    hidden = swiglu(dot(q_ref[...], gate_ref[0]), dot(q_ref[...], up_ref[0]))
    out = dot(hidden, down_ref[0]).astype(bf16)
    share_ref[...] = dot(out, proj_ref[...]).astype(bf16)
    gate_t_ref[...] = gate_ref[0].T
    up_t_ref[...] = up_ref[0].T


def descent_kernel(
    place_ref, keys_a, keys_b, scaled_a, scaled_b, gate_t_ref, up_t_ref, down_ref, kept_ref, given_ref, sums
):
    core, pair = place_ref[0], place_ref[1]
    part = down_ref.shape[1] // PAIR
    half = part // CORES
    units = pl.ds(pl.multiple_of(pair * part, part), part)
    keys = jnp.concatenate([keys_a[...], keys_b[...]], axis=0)
    scaled = jnp.concatenate([scaled_a[...], scaled_b[...]], axis=0)
    gating = dot(gate_t_ref[units, :], keys, (1, 1))
    lifted = dot(up_t_ref[units, :], keys, (1, 1))
    backward = dot(down_ref[0, units, :], scaled, (1, 1))
    s = jax.nn.sigmoid(gating)
    activated = gating * s
    hidden = (activated * lifted).astype(bf16)
    gate_back = (backward * lifted * s * (1.0 + gating * (1.0 - s))).astype(bf16)
    up_back = (backward * activated).astype(bf16)
    sums[0] = dot(gate_back, keys)
    sums[1] = dot(up_back, keys)
    sums[2] = dot(hidden, scaled)
    mine = pl.ds(pl.multiple_of(core * half, half), half)
    others = pl.ds(pl.multiple_of((1 - core) * half, half), half)
    for m in range(3):
        kept_ref[m * half : (m + 1) * half] = sums[m, mine, :]
        given_ref[m * half : (m + 1) * half] = sums[m, others, :].astype(bf16)


def second_kernel(
    place_ref, own_ref, other_ref, q_ref, gate_t_ref, up_t_ref, down_ref, proj_ref, first_ref, share_ref, work
):
    core = place_ref[0]
    width = q_ref.shape[1]
    half = width // PAIR // CORES
    piece = 3 * half // LOW
    step = math.gcd(piece, half)
    for low in range(LOW):
        for pair in range(PAIR):
            for row in range(0, piece, step):
                m, line = divmod(low * piece + row, half)
                base = pair * CORES * half + line
                mine = pl.multiple_of(base + core * half, step)
                others = pl.multiple_of(base + (1 - core) * half, step)
                at = (low * PAIR + pair) * piece + row
                work[m, pl.ds(mine, step), :] = own_ref[at : at + step]
                work[m, pl.ds(others, step), :] = other_ref[at : at + step]
    for m in range(3):
        widened = work[m].astype(f32)
        magnitude = jnp.sqrt(jnp.sum(widened * widened, keepdims=True)) + 1e-07
        work[m] = (widened / magnitude).astype(bf16)
    for step in range(NS_ITERS):
        for m in range(3):
            current = work[m]
            gram = dot(current, current, (1, 1)).astype(bf16)
            square = dot(gram, gram)
            polynomial = (second_coeff * gram.astype(f32) + third_coeff * square).astype(bf16)
            mixed = dot(polynomial, current)
            work[m] = (first_coeff * current.astype(f32) + mixed).astype(bf16)

    def updated(memory, m):
        return (memory.astype(f32) + step_scale * work[m].astype(f32)).astype(bf16)

    q = q_ref[...]
    gating = dot(q, updated(gate_t_ref[...], 0), (1, 1))
    lifted = dot(q, updated(up_t_ref[...], 1), (1, 1))
    out = dot(swiglu(gating, lifted), updated(down_ref[0], 2)).astype(bf16)
    share_ref[:, :width] = first_ref[...]
    share_ref[:, width:] = dot(out, proj_ref[...]).astype(bf16)


def local(kernel, outs, n_in, scalars, scratch, flops):
    whole = pl.BlockSpec(memory_space=pltpu.VMEM)
    smem = pl.BlockSpec(memory_space=pltpu.SMEM)
    return pl.pallas_call(
        kernel,
        out_shape=[jax.ShapeDtypeStruct(shape, kind) for shape, kind in outs],
        in_specs=[smem] * scalars + [whole] * n_in,
        out_specs=[whole] * len(outs),
        scratch_shapes=scratch,
        compiler_params=pltpu.CompilerParams(vmem_limit_bytes=VMEM_BYTES),
        cost_estimate=pl.CostEstimate(flops=flops, bytes_accessed=3 << 20, transcendentals=0),
    )


def on_device(q_first, keys, values, q_second, rates, gate_memory, up_memory, down_memory, out_proj):
    core = lax.axis_index("core")
    pair = lax.axis_index("pair")
    place = jnp.stack([core, pair]).astype(jnp.int32)
    tokens, width = keys.shape
    unit = width * width

    keys_next = lax.ppermute(keys, "pair", SWAP)
    scaled = (rates[0][:, None] * values.astype(f32)).astype(bf16)
    scaled_next = lax.ppermute(scaled, "pair", SWAP)
    first_share, gate_t, up_t = local(
        first_kernel,
        [((tokens, width), bf16), ((width, width), bf16), ((width, width), bf16)],
        5,
        0,
        [],
        8 * tokens * unit,
    )(q_first, gate_memory, up_memory, down_memory, out_proj)
    rows = 3 * width // PAIR // CORES
    kept, given = local(
        descent_kernel,
        [((rows, width), f32), ((rows, width), bf16)],
        7,
        1,
        [pltpu.VMEM((3, width // PAIR, width), f32)],
        12 * tokens * unit,
    )(place, keys, keys_next, scaled, scaled_next, gate_t, up_t, down_memory)
    taken = lax.all_gather(given, "core", axis=0, tiled=False)
    taken = lax.dynamic_index_in_dim(taken, 1 - core, 0, keepdims=False)
    pieces = (kept + taken.astype(f32)).astype(bf16)
    pieces = lax.all_to_all(pieces, ("low", "high"), 0, 0, tiled=True).reshape(HIGH * LOW, -1, width)
    summed = jnp.sum(pieces.astype(f32), axis=0).astype(bf16)
    groups = lax.all_gather(summed, ("far", "high"), axis=0, tiled=False)
    groups = groups.reshape((FAR, HIGH) + summed.shape)
    summed = jnp.sum(groups.astype(f32), axis=0).astype(bf16).reshape(-1, width)
    own = lax.all_gather(summed, ("low", "pair"), axis=0, tiled=True)
    other = lax.ppermute(own, "core", SWAP)
    (share,) = local(
        second_kernel,
        [((tokens, 2 * width), bf16)],
        8,
        1,
        [pltpu.VMEM((3, width, width), bf16)],
        36 * width * unit,
    )(place, own, other, q_second, gate_t, up_t, down_memory, out_proj, first_share)
    shares = lax.all_to_all(share, ("x", "y"), 0, 0, tiled=True)
    shares = shares.reshape(SIDE * SIDE, -1, 2 * width)
    return jnp.sum(shares.astype(f32), axis=0).astype(bf16)


def solution(mesh):
    fine = Mesh(
        mesh.devices.reshape(FAR, HIGH, LOW, PAIR, CORES, SIDE, SIDE),
        ("far", "high", "low", "pair", "core", "x", "y"),
    )
    seq, head = ("far", "high", "low", "pair", "core"), ("x", "y")
    in_specs = (
        P(seq, head),
        P(seq, head),
        P(seq, head),
        P(seq, head),
        P(head, seq),
        P(head, None, None),
        P(head, None, None),
        P(head, None, None),
        P(head, None),
    )
    out_specs = P(seq + head, None)
    return jax.shard_map(
        on_device, mesh=fine, in_specs=in_specs, out_specs=out_specs, check_vma=False
    )
```

```python
import math

import jax
import jax.numpy as jnp
from jax import lax
from jax.experimental import pallas as pl
from jax.experimental.pallas import tpu as pltpu
from jax.sharding import Mesh
from jax.sharding import PartitionSpec as P

NS_ITERS = 2
FAR, HIGH, LOW, PAIR, CORES, SIDE = 4, 2, 2, 2, 2, 4
VMEM_BYTES = 48 * 1024 * 1024

first_coeff = 3.4445
second_coeff = -4.775
third_coeff = 2.0315
step_scale = 0.5

f32 = jnp.float32
bf16 = jnp.bfloat16
SWAP = [(0, 1), (1, 0)]


def dot(a, b, contract=(1, 0)):
    return lax.dot_general(a, b, ((contract[:1], contract[1:]), ((), ())), preferred_element_type=f32)


def swiglu(gating, lifted):
    return (gating * jax.nn.sigmoid(gating) * lifted).astype(bf16)


def first_kernel(q_ref, gate_ref, up_ref, down_ref, proj_ref, share_ref, gate_t_ref, up_t_ref):
    hidden = swiglu(dot(q_ref[...], gate_ref[0]), dot(q_ref[...], up_ref[0]))
    out = dot(hidden, down_ref[0]).astype(bf16)
    share_ref[...] = dot(out, proj_ref[...]).astype(bf16)
    gate_t_ref[...] = gate_ref[0].T
    up_t_ref[...] = up_ref[0].T


def descent_kernel(place_ref, tokens_ref, gate_ref, up_ref, down_ref, kept_ref, given_ref, sums):
    core, pair = place_ref[0], place_ref[1]
    rows = tokens_ref.shape[0] // (2 * PAIR)
    part = down_ref.shape[1] // PAIR
    half = part // CORES
    units = pl.ds(pl.multiple_of(pair * part, part), part)
    keys = jnp.concatenate([tokens_ref[2 * i * rows : (2 * i + 1) * rows] for i in range(PAIR)], axis=0)
    scaled = jnp.concatenate([tokens_ref[(2 * i + 1) * rows : (2 * i + 2) * rows] for i in range(PAIR)], axis=0)
    gating = dot(gate_ref[0, :, units].T, keys, (1, 1))
    lifted = dot(up_ref[0, :, units].T, keys, (1, 1))
    backward = dot(down_ref[0, units, :], scaled, (1, 1))
    s = jax.nn.sigmoid(gating)
    activated = gating * s
    hidden = (activated * lifted).astype(bf16)
    gate_back = (backward * lifted * s * (1.0 + gating * (1.0 - s))).astype(bf16)
    up_back = (backward * activated).astype(bf16)
    sums[0] = dot(gate_back, keys)
    sums[1] = dot(up_back, keys)
    sums[2] = dot(hidden, scaled)
    mine = pl.ds(pl.multiple_of(core * half, half), half)
    others = pl.ds(pl.multiple_of((1 - core) * half, half), half)
    for m in range(3):
        kept_ref[m * half : (m + 1) * half] = sums[m, mine, :]
        given_ref[m * half : (m + 1) * half] = sums[m, others, :].astype(bf16)


def second_kernel(
    place_ref, own_ref, other_ref, q_ref, gate_t_ref, up_t_ref, down_ref, proj_ref, first_ref, share_ref, work
):
    core = place_ref[0]
    width = q_ref.shape[1]
    half = width // PAIR // CORES
    piece = 3 * half // LOW
    step = math.gcd(piece, half)
    blocks = []
    for at in range(0, PAIR * 3 * half, step):
        source, row = divmod(at, piece)
        low, pair = divmod(source, PAIR)
        m, line = divmod(low * piece + row, half)
        blocks.append((at, m, pair * CORES * half + line))
    squares = [jnp.zeros((8, width), f32) for m in range(3)]
    for ref in (own_ref, other_ref):
        for at, m, base in blocks:
            widened = ref[at : at + step].astype(f32)
            squares[m] += jnp.sum((widened * widened).reshape(step // 8, 8, width), axis=0)
    scales = [1.0 / (jnp.sqrt(jnp.sum(square, keepdims=True)) + 1e-07) for square in squares]
    for ref, owner in ((own_ref, core), (other_ref, 1 - core)):
        for at, m, base in blocks:
            rows = pl.ds(pl.multiple_of(base + owner * half, step), step)
            work[m, rows, :] = (ref[at : at + step].astype(f32) * scales[m]).astype(bf16)
    for step in range(NS_ITERS):
        for m in range(3):
            current = work[m]
            gram = dot(current, current, (1, 1)).astype(bf16)
            square = dot(gram, gram)
            polynomial = (second_coeff * gram.astype(f32) + third_coeff * square).astype(bf16)
            mixed = dot(polynomial, current)
            work[m] = (first_coeff * current.astype(f32) + mixed).astype(bf16)

    def updated(memory, m):
        return (memory.astype(f32) + step_scale * work[m].astype(f32)).astype(bf16)

    q = q_ref[...]
    gating = dot(q, updated(gate_t_ref[...], 0), (1, 1))
    lifted = dot(q, updated(up_t_ref[...], 1), (1, 1))
    out = dot(swiglu(gating, lifted), updated(down_ref[0], 2)).astype(bf16)
    share_ref[:, :width] = first_ref[...]
    share_ref[:, width:] = dot(out, proj_ref[...]).astype(bf16)


def local(kernel, outs, n_in, scalars, scratch, flops):
    whole = pl.BlockSpec(memory_space=pltpu.VMEM)
    smem = pl.BlockSpec(memory_space=pltpu.SMEM)
    return pl.pallas_call(
        kernel,
        out_shape=[jax.ShapeDtypeStruct(shape, kind) for shape, kind in outs],
        in_specs=[smem] * scalars + [whole] * n_in,
        out_specs=[whole] * len(outs),
        scratch_shapes=scratch,
        compiler_params=pltpu.CompilerParams(vmem_limit_bytes=VMEM_BYTES),
        cost_estimate=pl.CostEstimate(flops=flops, bytes_accessed=3 << 20, transcendentals=0),
    )


def on_device(q_first, keys, values, q_second, rates, gate_memory, up_memory, down_memory, out_proj):
    core = lax.axis_index("core")
    pair = lax.axis_index("pair")
    place = jnp.stack([core, pair]).astype(jnp.int32)
    tokens, width = keys.shape
    unit = width * width

    scaled = (rates[0][:, None] * values.astype(f32)).astype(bf16)
    gathered = lax.all_gather(jnp.concatenate([keys, scaled], axis=0), "pair", axis=0, tiled=True)
    rows = 3 * width // PAIR // CORES
    kept, given = local(
        descent_kernel,
        [((rows, width), f32), ((rows, width), bf16)],
        4,
        1,
        [pltpu.VMEM((3, width // PAIR, width), f32)],
        12 * tokens * unit,
    )(place, gathered, gate_memory, up_memory, down_memory)
    taken = lax.all_gather(given, "core", axis=0, tiled=False)
    taken = lax.dynamic_index_in_dim(taken, 1 - core, 0, keepdims=False)
    pieces = (kept + taken.astype(f32)).astype(bf16)
    pieces = lax.all_to_all(pieces, ("low", "high"), 0, 0, tiled=True).reshape(HIGH * LOW, -1, width)
    summed = jnp.sum(pieces.astype(f32), axis=0).astype(bf16)
    groups = lax.all_gather(summed, ("far", "high"), axis=0, tiled=False)
    groups = groups.reshape((FAR, HIGH) + summed.shape)
    summed = jnp.sum(groups.astype(f32), axis=0).astype(bf16).reshape(-1, width)
    own = lax.all_gather(summed, ("low", "pair"), axis=0, tiled=True)
    other = lax.ppermute(own, "core", SWAP)
    first_share, gate_t, up_t = local(
        first_kernel,
        [((tokens, width), bf16), ((width, width), bf16), ((width, width), bf16)],
        5,
        0,
        [],
        8 * tokens * unit,
    )(q_first, gate_memory, up_memory, down_memory, out_proj)
    (share,) = local(
        second_kernel,
        [((tokens, 2 * width), bf16)],
        8,
        1,
        [pltpu.VMEM((3, width, width), bf16)],
        36 * width * unit,
    )(place, own, other, q_second, gate_t, up_t, down_memory, out_proj, first_share)
    shares = lax.all_to_all(share, ("x", "y"), 0, 0, tiled=True)
    shares = shares.reshape(SIDE * SIDE, -1, 2 * width)
    return jnp.sum(shares.astype(f32), axis=0).astype(bf16)


def solution(mesh):
    fine = Mesh(
        mesh.devices.reshape(FAR, HIGH, LOW, PAIR, CORES, SIDE, SIDE),
        ("far", "high", "low", "pair", "core", "x", "y"),
    )
    seq, head = ("far", "high", "low", "pair", "core"), ("x", "y")
    in_specs = (
        P(seq, head),
        P(seq, head),
        P(seq, head),
        P(seq, head),
        P(head, seq),
        P(head, None, None),
        P(head, None, None),
        P(head, None, None),
        P(head, None),
    )
    out_specs = P(seq + head, None)
    return jax.shard_map(
        on_device, mesh=fine, in_specs=in_specs, out_specs=out_specs, check_vma=False
    )
```

```python
import math

import jax
import jax.numpy as jnp
from jax import lax
from jax.experimental import pallas as pl
from jax.experimental.pallas import tpu as pltpu
from jax.sharding import Mesh
from jax.sharding import PartitionSpec as P

NS_ITERS = 2
TOP, FAR, HIGH, LOW, PAIR, CORES, SIDE = 2, 2, 2, 2, 2, 2, 4
VMEM_BYTES = 48 * 1024 * 1024

first_coeff = 3.4445
second_coeff = -4.775
third_coeff = 2.0315
step_scale = 0.5

f32 = jnp.float32
bf16 = jnp.bfloat16
SWAP = [(0, 1), (1, 0)]


def dot(a, b, contract=(1, 0)):
    return lax.dot_general(a, b, ((contract[:1], contract[1:]), ((), ())), preferred_element_type=f32)


def swiglu(gating, lifted):
    return (gating * jax.nn.sigmoid(gating) * lifted).astype(bf16)


def first_kernel(q_ref, gate_ref, up_ref, down_ref, proj_ref, share_ref, gate_t_ref, up_t_ref):
    hidden = swiglu(dot(q_ref[...], gate_ref[0]), dot(q_ref[...], up_ref[0]))
    out = dot(hidden, down_ref[0]).astype(bf16)
    share_ref[...] = dot(out, proj_ref[...]).astype(bf16)
    gate_t_ref[...] = gate_ref[0].T
    up_t_ref[...] = up_ref[0].T


def descent_kernel(place_ref, tokens_ref, gate_ref, up_ref, down_ref, kept_ref, given_ref, sums):
    core, pair = place_ref[0], place_ref[1]
    rows = tokens_ref.shape[0] // (2 * PAIR)
    part = down_ref.shape[1] // PAIR
    half = part // CORES
    units = pl.ds(pl.multiple_of(pair * part, part), part)
    keys = jnp.concatenate([tokens_ref[2 * i * rows : (2 * i + 1) * rows] for i in range(PAIR)], axis=0)
    scaled = jnp.concatenate([tokens_ref[(2 * i + 1) * rows : (2 * i + 2) * rows] for i in range(PAIR)], axis=0)
    gating = dot(gate_ref[0, :, units].T, keys, (1, 1))
    lifted = dot(up_ref[0, :, units].T, keys, (1, 1))
    backward = dot(down_ref[0, units, :], scaled, (1, 1))
    s = jax.nn.sigmoid(gating)
    activated = gating * s
    hidden = (activated * lifted).astype(bf16)
    gate_back = (backward * lifted * s * (1.0 + gating * (1.0 - s))).astype(bf16)
    up_back = (backward * activated).astype(bf16)
    sums[0] = dot(gate_back, keys)
    sums[1] = dot(up_back, keys)
    sums[2] = dot(hidden, scaled)
    mine = pl.ds(pl.multiple_of(core * half, half), half)
    others = pl.ds(pl.multiple_of((1 - core) * half, half), half)
    for m in range(3):
        kept_ref[m * half : (m + 1) * half] = sums[m, mine, :]
        given_ref[m * half : (m + 1) * half] = sums[m, others, :].astype(bf16)


def second_kernel(
    place_ref, own_ref, other_ref, q_ref, gate_t_ref, up_t_ref, down_ref, proj_ref, first_ref, share_ref, work
):
    core = place_ref[0]
    width = q_ref.shape[1]
    half = width // PAIR // CORES
    piece = 3 * half // LOW
    step = math.gcd(piece, half)
    blocks = []
    for at in range(0, PAIR * 3 * half, step):
        source, row = divmod(at, piece)
        low, pair = divmod(source, PAIR)
        m, line = divmod(low * piece + row, half)
        blocks.append((at, m, pair * CORES * half + line))
    squares = [jnp.zeros((8, width), f32) for m in range(3)]
    for ref in (own_ref, other_ref):
        for at, m, base in blocks:
            widened = ref[at : at + step].astype(f32)
            squares[m] += jnp.sum((widened * widened).reshape(step // 8, 8, width), axis=0)
    scales = [1.0 / (jnp.sqrt(jnp.sum(square, keepdims=True)) + 1e-07) for square in squares]
    for ref, owner in ((own_ref, core), (other_ref, 1 - core)):
        for at, m, base in blocks:
            rows = pl.ds(pl.multiple_of(base + owner * half, step), step)
            work[m, rows, :] = (ref[at : at + step].astype(f32) * scales[m]).astype(bf16)
    for step in range(NS_ITERS):
        for m in range(3):
            current = work[m]
            gram = dot(current, current, (1, 1)).astype(bf16)
            square = dot(gram, gram)
            polynomial = (second_coeff * gram.astype(f32) + third_coeff * square).astype(bf16)
            mixed = dot(polynomial, current)
            work[m] = (first_coeff * current.astype(f32) + mixed).astype(bf16)

    def updated(memory, m):
        return (memory.astype(f32) + step_scale * work[m].astype(f32)).astype(bf16)

    q = q_ref[...]
    gating = dot(q, updated(gate_t_ref[...], 0), (1, 1))
    lifted = dot(q, updated(up_t_ref[...], 1), (1, 1))
    out = dot(swiglu(gating, lifted), updated(down_ref[0], 2)).astype(bf16)
    share_ref[:, :width] = first_ref[...]
    share_ref[:, width:] = dot(out, proj_ref[...]).astype(bf16)


def local(kernel, outs, n_in, scalars, scratch, flops):
    whole = pl.BlockSpec(memory_space=pltpu.VMEM)
    smem = pl.BlockSpec(memory_space=pltpu.SMEM)
    return pl.pallas_call(
        kernel,
        out_shape=[jax.ShapeDtypeStruct(shape, kind) for shape, kind in outs],
        in_specs=[smem] * scalars + [whole] * n_in,
        out_specs=[whole] * len(outs),
        scratch_shapes=scratch,
        compiler_params=pltpu.CompilerParams(vmem_limit_bytes=VMEM_BYTES),
        cost_estimate=pl.CostEstimate(flops=flops, bytes_accessed=3 << 20, transcendentals=0),
    )


def on_device(q_first, keys, values, q_second, rates, gate_memory, up_memory, down_memory, out_proj):
    core = lax.axis_index("core")
    pair = lax.axis_index("pair")
    place = jnp.stack([core, pair]).astype(jnp.int32)
    tokens, width = keys.shape
    unit = width * width

    scaled = (rates[0][:, None] * values.astype(f32)).astype(bf16)
    gathered = lax.all_gather(jnp.concatenate([keys, scaled], axis=0), "pair", axis=0, tiled=True)
    rows = 3 * width // PAIR // CORES
    kept, given = local(
        descent_kernel,
        [((rows, width), f32), ((rows, width), bf16)],
        4,
        1,
        [pltpu.VMEM((3, width // PAIR, width), f32)],
        12 * tokens * unit,
    )(place, gathered, gate_memory, up_memory, down_memory)
    taken = lax.all_gather(given, "core", axis=0, tiled=False)
    taken = lax.dynamic_index_in_dim(taken, 1 - core, 0, keepdims=False)
    pieces = (kept + taken.astype(f32)).astype(bf16)
    pieces = lax.all_to_all(pieces, ("low", "high"), 0, 0, tiled=True).reshape(HIGH * LOW, -1, width)
    far = lax.axis_index("far")
    halves = jnp.sum(pieces.astype(f32), axis=0).reshape(FAR, -1, width)
    taken = lax.all_gather(
        lax.dynamic_index_in_dim(halves, 1 - far, 0, keepdims=False).astype(bf16), "far", axis=0, tiled=False
    )
    taken = lax.dynamic_index_in_dim(taken, 1 - far, 0, keepdims=False)
    summed = (lax.dynamic_index_in_dim(halves, far, 0, keepdims=False) + taken.astype(f32)).astype(bf16)
    groups = lax.all_gather(summed, ("top", "far", "high", "core"), axis=0, tiled=False)
    groups = groups.reshape((TOP, FAR, HIGH, CORES) + summed.shape)
    groups = lax.dynamic_index_in_dim(groups, core, 3, keepdims=False)
    summed = jnp.sum(groups.astype(f32), axis=0).astype(bf16)
    summed = summed.transpose(1, 0, 2, 3).reshape(-1, width)
    own = lax.all_gather(summed, ("low", "pair"), axis=0, tiled=True)
    other = lax.ppermute(own, "core", SWAP)
    first_share, gate_t, up_t = local(
        first_kernel,
        [((tokens, width), bf16), ((width, width), bf16), ((width, width), bf16)],
        5,
        0,
        [],
        8 * tokens * unit,
    )(q_first, gate_memory, up_memory, down_memory, out_proj)
    (share,) = local(
        second_kernel,
        [((tokens, 2 * width), bf16)],
        8,
        1,
        [pltpu.VMEM((3, width, width), bf16)],
        36 * width * unit,
    )(place, own, other, q_second, gate_t, up_t, down_memory, out_proj, first_share)
    shares = lax.all_to_all(share, ("x", "y"), 0, 0, tiled=True)
    shares = shares.reshape(SIDE * SIDE, -1, 2 * width)
    return jnp.sum(shares.astype(f32), axis=0).astype(bf16)


def solution(mesh):
    fine = Mesh(
        mesh.devices.reshape(TOP, FAR, HIGH, LOW, PAIR, CORES, SIDE, SIDE),
        ("top", "far", "high", "low", "pair", "core", "x", "y"),
    )
    seq, head = ("top", "far", "high", "low", "pair", "core"), ("x", "y")
    in_specs = (
        P(seq, head),
        P(seq, head),
        P(seq, head),
        P(seq, head),
        P(head, seq),
        P(head, None, None),
        P(head, None, None),
        P(head, None, None),
        P(head, None),
    )
    out_specs = P(seq + head, None)
    return jax.shard_map(
        on_device, mesh=fine, in_specs=in_specs, out_specs=out_specs, check_vma=False
    )
```

```python
import math

import jax
import jax.numpy as jnp
from jax import lax
from jax.experimental import pallas as pl
from jax.experimental.pallas import tpu as pltpu
from jax.sharding import Mesh
from jax.sharding import PartitionSpec as P

NS_ITERS = 2
TOP, FAR, HIGH, LOW, PAIR, CORES, SIDE = 2, 2, 2, 2, 2, 2, 4
VMEM_BYTES = 48 * 1024 * 1024

first_coeff = 3.4445
second_coeff = -4.775
third_coeff = 2.0315
step_scale = 0.5

f32 = jnp.float32
bf16 = jnp.bfloat16
SWAP = [(0, 1), (1, 0)]


def dot(a, b, contract=(1, 0)):
    return lax.dot_general(a, b, ((contract[:1], contract[1:]), ((), ())), preferred_element_type=f32)


def swiglu(gating, lifted):
    return (gating * jax.nn.sigmoid(gating) * lifted).astype(bf16)


def first_kernel(q_ref, gate_ref, up_ref, down_ref, proj_ref, share_ref, gate_t_ref, up_t_ref):
    hidden = swiglu(dot(q_ref[...], gate_ref[0]), dot(q_ref[...], up_ref[0]))
    out = dot(hidden, down_ref[0]).astype(bf16)
    share_ref[...] = dot(out, proj_ref[...]).astype(bf16)
    gate_t_ref[...] = gate_ref[0].T
    up_t_ref[...] = up_ref[0].T


def descent_kernel(place_ref, tokens_ref, gate_ref, up_ref, down_ref, kept_ref, given_ref, sums):
    core, pair = place_ref[0], place_ref[1]
    rows = tokens_ref.shape[0] // (2 * PAIR)
    part = down_ref.shape[1] // PAIR
    half = part // CORES
    units = pl.ds(pl.multiple_of(pair * part, part), part)
    keys = jnp.concatenate([tokens_ref[2 * i * rows : (2 * i + 1) * rows] for i in range(PAIR)], axis=0)
    scaled = jnp.concatenate([tokens_ref[(2 * i + 1) * rows : (2 * i + 2) * rows] for i in range(PAIR)], axis=0)
    gating = dot(gate_ref[0, :, units].T, keys, (1, 1))
    lifted = dot(up_ref[0, :, units].T, keys, (1, 1))
    backward = dot(down_ref[0, units, :], scaled, (1, 1))
    s = jax.nn.sigmoid(gating)
    activated = gating * s
    hidden = (activated * lifted).astype(bf16)
    gate_back = (backward * lifted * s * (1.0 + gating * (1.0 - s))).astype(bf16)
    up_back = (backward * activated).astype(bf16)
    sums[0] = dot(gate_back, keys)
    sums[1] = dot(up_back, keys)
    sums[2] = dot(hidden, scaled)
    mine = pl.ds(pl.multiple_of(core * half, half), half)
    others = pl.ds(pl.multiple_of((1 - core) * half, half), half)
    for m in range(3):
        kept_ref[m * half : (m + 1) * half] = sums[m, mine, :]
        given_ref[m * half : (m + 1) * half] = sums[m, others, :].astype(bf16)


def second_kernel(
    place_ref, own_ref, other_ref, q_ref, gate_t_ref, up_t_ref, down_ref, proj_ref, first_ref, share_ref, work
):
    core = place_ref[0]
    width = q_ref.shape[1]
    half = width // PAIR // CORES
    piece = 3 * half // LOW
    share = piece // FAR // HIGH
    step = math.gcd(share, half)
    blocks = []
    for at in range(0, PAIR * 3 * half, step):
        source, row = divmod(at, piece)
        low, pair = divmod(source, PAIR)
        far, high = divmod(row // share, HIGH)
        m, line = divmod(((low * HIGH + high) * FAR + far) * share + row % share, half)
        blocks.append((at, m, pair * CORES * half + line))
    squares = [jnp.zeros((8, width), f32) for m in range(3)]
    for ref in (own_ref, other_ref):
        for at, m, base in blocks:
            widened = ref[at : at + step].astype(f32)
            squares[m] += jnp.sum((widened * widened).reshape(step // 8, 8, width), axis=0)
    scales = [1.0 / (jnp.sqrt(jnp.sum(square, keepdims=True)) + 1e-07) for square in squares]
    for ref, owner in ((own_ref, core), (other_ref, 1 - core)):
        for at, m, base in blocks:
            rows = pl.ds(pl.multiple_of(base + owner * half, step), step)
            work[m, rows, :] = (ref[at : at + step].astype(f32) * scales[m]).astype(bf16)
    for step in range(NS_ITERS):
        for m in range(3):
            current = work[m]
            gram = dot(current, current, (1, 1)).astype(bf16)
            square = dot(gram, gram)
            polynomial = (second_coeff * gram.astype(f32) + third_coeff * square).astype(bf16)
            mixed = dot(polynomial, current)
            work[m] = (first_coeff * current.astype(f32) + mixed).astype(bf16)

    def updated(memory, m):
        return (memory.astype(f32) + step_scale * work[m].astype(f32)).astype(bf16)

    q = q_ref[...]
    gating = dot(q, updated(gate_t_ref[...], 0), (1, 1))
    lifted = dot(q, updated(up_t_ref[...], 1), (1, 1))
    out = dot(swiglu(gating, lifted), updated(down_ref[0], 2)).astype(bf16)
    share_ref[:, :width] = first_ref[...]
    share_ref[:, width:] = dot(out, proj_ref[...]).astype(bf16)


def local(kernel, outs, n_in, scalars, scratch, flops):
    whole = pl.BlockSpec(memory_space=pltpu.VMEM)
    smem = pl.BlockSpec(memory_space=pltpu.SMEM)
    return pl.pallas_call(
        kernel,
        out_shape=[jax.ShapeDtypeStruct(shape, kind) for shape, kind in outs],
        in_specs=[smem] * scalars + [whole] * n_in,
        out_specs=[whole] * len(outs),
        scratch_shapes=scratch,
        compiler_params=pltpu.CompilerParams(vmem_limit_bytes=VMEM_BYTES),
        cost_estimate=pl.CostEstimate(flops=flops, bytes_accessed=3 << 20, transcendentals=0),
    )


def on_device(q_first, keys, values, q_second, rates, gate_memory, up_memory, down_memory, out_proj):
    core = lax.axis_index("core")
    pair = lax.axis_index("pair")
    place = jnp.stack([core, pair]).astype(jnp.int32)
    tokens, width = keys.shape
    unit = width * width

    scaled = (rates[0][:, None] * values.astype(f32)).astype(bf16)
    gathered = lax.all_gather(jnp.concatenate([keys, scaled], axis=0), "pair", axis=0, tiled=True)
    rows = 3 * width // PAIR // CORES
    kept, given = local(
        descent_kernel,
        [((rows, width), f32), ((rows, width), bf16)],
        4,
        1,
        [pltpu.VMEM((3, width // PAIR, width), f32)],
        12 * tokens * unit,
    )(place, gathered, gate_memory, up_memory, down_memory)
    taken = lax.all_gather(given, "core", axis=0, tiled=False)
    taken = jnp.where(core == 0, taken[1], taken[0])
    pieces = (kept + taken.astype(f32)).astype(bf16)
    pieces = lax.all_to_all(pieces, ("low", "high"), 0, 0, tiled=True).reshape(HIGH * LOW, -1, width)
    far = lax.axis_index("far")
    halves = jnp.sum(pieces.astype(f32), axis=0).reshape(FAR, -1, width)
    taken = lax.all_gather(
        jnp.where(far == 0, halves[1], halves[0]).astype(bf16), "far", axis=0, tiled=False
    )
    taken = jnp.where(far == 0, taken[1], taken[0])
    summed = (jnp.where(far == 0, halves[0], halves[1]) + taken.astype(f32)).astype(bf16)
    groups = lax.all_gather(summed, ("top", "far", "high", "core"), axis=0, tiled=False)
    groups = groups.reshape((TOP, FAR, HIGH, CORES) + summed.shape)
    groups = jnp.where(core == 0, groups[:, :, :, 0], groups[:, :, :, 1])
    summed = jnp.sum(groups.astype(f32), axis=0).astype(bf16)
    summed = summed.reshape(-1, width)
    own = lax.all_gather(summed, ("low", "pair"), axis=0, tiled=True)
    other = lax.ppermute(own, "core", SWAP)
    first_share, gate_t, up_t = local(
        first_kernel,
        [((tokens, width), bf16), ((width, width), bf16), ((width, width), bf16)],
        5,
        0,
        [],
        8 * tokens * unit,
    )(q_first, gate_memory, up_memory, down_memory, out_proj)
    (share,) = local(
        second_kernel,
        [((tokens, 2 * width), bf16)],
        8,
        1,
        [pltpu.VMEM((3, width, width), bf16)],
        36 * width * unit,
    )(place, own, other, q_second, gate_t, up_t, down_memory, out_proj, first_share)
    shares = lax.all_to_all(share, ("x", "y"), 0, 0, tiled=True)
    shares = shares.reshape(SIDE * SIDE, -1, 2 * width)
    return jnp.sum(shares.astype(f32), axis=0).astype(bf16)


def solution(mesh):
    fine = Mesh(
        mesh.devices.reshape(TOP, FAR, HIGH, LOW, PAIR, CORES, SIDE, SIDE),
        ("top", "far", "high", "low", "pair", "core", "x", "y"),
    )
    seq, head = ("top", "far", "high", "low", "pair", "core"), ("x", "y")
    in_specs = (
        P(seq, head),
        P(seq, head),
        P(seq, head),
        P(seq, head),
        P(head, seq),
        P(head, None, None),
        P(head, None, None),
        P(head, None, None),
        P(head, None),
    )
    out_specs = P(seq + head, None)
    return jax.shard_map(
        on_device, mesh=fine, in_specs=in_specs, out_specs=out_specs, check_vma=False
    )
```
